32 devices in a mesh: groups: 2 (over x), row: 16 (over z, y, core).
Axes of the slice: x: 2, y: 2, z: 4, core: 2. Of those that a mesh axis runs over, the one named last changes fastest.
Arguments:
- alignment_embedding: bfloat16 [64, 256, 256], P('groups', 'row'), parts along dimension 0, may hold values from -6 to 6
- standardize_scaling: float32 [256], replicated, may hold values from 0.1 to 1.9
- standardize_offset: float32 [256], replicated, may hold values from -3 to 3
- first_factor_matrix: bfloat16 [256, 32], replicated, may hold values from -0.375 to 0.375
- first_factor_offset: float32 [32], replicated, may hold values from -3 to 3
- second_factor_matrix: bfloat16 [256, 32], replicated, may hold values from -0.375 to 0.375
- second_factor_offset: float32 [32], replicated, may hold values from -3 to 3
- final_matrix: bfloat16 [1024, 128], replicated, may hold values from -1.796875 to 1.796875
- final_offset: float32 [128], replicated, may hold values from -3 to 3
- pairwise_embedding: bfloat16 [512, 256, 128], P(('groups', 'row')), parts along dimension 0, may hold values from -6 to 6
Outputs:
- pair_out: bfloat16 [512, 256, 128], P(('groups', 'row')), parts along dimension 0
The draws below stay inside these ranges and needn't reach their ends.
There are 2 independent parts, one for each index of `groups`. The reference program is written for one: setup_inputs(seed, part) draws one part's arguments, and reference() takes and returns one part's arrays. A program takes and returns all parts, laid end to end along the dimension named above; an argument that names none is the same for every part. Nothing has to cross between parts.
All inputs are finite; a program needn't handle non-finite values.
Results may differ from the reference program's by a relative error of at most 0.0056.
Values may be sent and summed in bfloat16 or wider, within the bound.
A program may use at most 192 MiB of HBM per device.

```python
import jax
import jax.numpy as jnp
from jax import lax

ALIGNMENT_DEPTH = 256
HIDDEN_WIDTH = 32
CZ = 128
ALIGNED_HOMOLOGS = 32
RES_DEV = 16
CHAIN_LENGTH = 256
N_ROW = 16


def level_of(key, extent, pieces, least, top_value):
    level = 1.0
    for dim, parts in pieces:
        steps = jax.random.uniform(jax.random.fold_in(jax.random.fold_in(key, 6), dim), (parts,), jnp.float32, least / len(pieces), top_value / len(pieces))
        level = level * jnp.repeat(jnp.exp(steps), extent[dim] // parts).reshape((-1,) + (1,) * (len(extent) - 1 - dim))
    return level


def bell_draw(own_key, shape, width, most, cuts=(), kind=jnp.bfloat16):
    loudness = level_of(own_key, shape, cuts, -0.22, 0.18) if cuts else 1.0
    result = jax.random.normal(own_key, shape, jnp.float32) * width * loudness
    return jnp.minimum(jnp.maximum(result, -most), most).astype(kind)


def setup_inputs(seed: int = 0, part: int = 0) -> dict:
    key_list = jax.random.split(jax.random.key(seed), 11)
    part_keys = jax.random.split(jax.random.fold_in(key_list[10], part), 11)
    return {
        "alignment_embedding": bell_draw(part_keys[0], (ALIGNED_HOMOLOGS, CHAIN_LENGTH, ALIGNMENT_DEPTH), 1.0, 6.0, ((1, 16),)),
        "standardize_scaling": jnp.clip(1.0 + 0.18 * jax.random.normal(key_list[1], (ALIGNMENT_DEPTH,), jnp.float32), 0.1, 1.9),
        "standardize_offset": bell_draw(key_list[2], (ALIGNMENT_DEPTH,), 0.5, 3.0, (), jnp.float32),
        "first_factor_matrix": bell_draw(key_list[3], (ALIGNMENT_DEPTH, HIDDEN_WIDTH), ALIGNMENT_DEPTH ** -0.5, 0.375),
        "first_factor_offset": bell_draw(key_list[4], (HIDDEN_WIDTH,), 0.5, 3.0, (), jnp.float32),
        "second_factor_matrix": bell_draw(key_list[5], (ALIGNMENT_DEPTH, HIDDEN_WIDTH), ALIGNMENT_DEPTH ** -0.5, 0.375),
        "second_factor_offset": bell_draw(key_list[6], (HIDDEN_WIDTH,), 0.5, 3.0, (), jnp.float32),
        "final_matrix": bell_draw(key_list[7], (HIDDEN_WIDTH * HIDDEN_WIDTH, CZ), 0.3, 1.796875),
        "final_offset": bell_draw(key_list[8], (CZ,), 0.5, 3.0, (), jnp.float32),
        "pairwise_embedding": bell_draw(part_keys[9], (CHAIN_LENGTH, CHAIN_LENGTH, CZ), 1.0, 6.0, ((0, 16),)),
    }


def standardize_embedding(values, standardize_scaling, standardize_offset):
    x = values.astype(jnp.float32)
    mean = lax.optimization_barrier(jnp.mean(x, axis=-1, keepdims=True))
    var = lax.optimization_barrier(jnp.mean((x - mean) * (x - mean), axis=-1, keepdims=True))
    return ((x - mean) * lax.rsqrt(var + 1e-05) * standardize_scaling + standardize_offset).astype(jnp.bfloat16)

def linear_map(standardized_alignment, coefficient_matrix, offset_vector):
    final_update = jnp.einsum('vot,tw->vow', standardized_alignment.astype(jnp.float32), coefficient_matrix.astype(jnp.float32))
    return (final_update + offset_vector).astype(jnp.bfloat16)

def reference(alignment_embedding, standardize_scaling, standardize_offset, first_factor_matrix, first_factor_offset, second_factor_matrix, second_factor_offset, final_matrix, final_offset, pairwise_embedding):
    standardized_alignment = standardize_embedding(alignment_embedding, standardize_scaling, standardize_offset)
    first_factor = linear_map(standardized_alignment, first_factor_matrix, first_factor_offset)
    second_factor = linear_map(standardized_alignment, second_factor_matrix, second_factor_offset)
    right_features = second_factor.astype(jnp.float32)

    def row_block(k):
        start = (k * RES_DEV).astype(jnp.int32)
        sequence_rows = lax.dynamic_slice_in_dim(first_factor, start, RES_DEV, 1).astype(jnp.float32)
        outer_product = jnp.einsum('kxd,kyr->xydr', sequence_rows, right_features) / float(ALIGNED_HOMOLOGS)
        outer_product = outer_product.astype(jnp.bfloat16).reshape(RES_DEV * CHAIN_LENGTH, HIDDEN_WIDTH * HIDDEN_WIDTH)
        update = jnp.dot(outer_product, final_matrix, preferred_element_type=jnp.float32) + final_offset
        update = update.reshape(RES_DEV, CHAIN_LENGTH, CZ)
        tile = lax.dynamic_slice_in_dim(pairwise_embedding, start, RES_DEV, 0).astype(jnp.float32)
        return (tile + update).astype(jnp.bfloat16)
    blocks = lax.map(row_block, jnp.arange(N_ROW, dtype=jnp.int32))
    return blocks.reshape(CHAIN_LENGTH, CHAIN_LENGTH, CZ)
```

```python
import functools

import jax
import jax.numpy as jnp
from jax import lax
from jax.experimental import pallas as pl
from jax.experimental.pallas import tpu as pltpu
from jax.sharding import PartitionSpec as P

MESH = pl.DeviceIdType.MESH
LANES = 128


def kernel(
    n_row,
    x_ref,
    scale_ref,
    shift_ref,
    left_w_ref,
    left_b_ref,
    right_w_ref,
    right_b_ref,
    final_hbm,
    final_b_ref,
    pair_hbm,
    out_hbm,
    normed_ref,
    final_ref,
    final32_ref,
    folded_ref,
    turned_ref,
    rows_ref,
    cols_ref,
    pair_ref,
    out_ref,
    pair_sem,
    final_sem,
    out_sem,
    send_sem,
    recv_sem,
):
    depth, res, channels = x_ref.shape
    width = left_w_ref.shape[1]
    cz = final_b_ref.shape[0]
    pack = LANES // depth
    high = width // pack

    me = lax.axis_index("row")
    core = lax.rem(me, 2)
    y = lax.rem(me // 2, 2)
    z = me // 4
    nz = n_row // 4

    def place(z_, y_, core_):
        return z_ * 4 + y_ * 2 + core_

    steps = sorted(range(1, nz), key=lambda d: (min(d, nz - d), d))
    across = place(z, 1 - y, core)
    sibling = place(z, y, 1 - core)
    line = [place(lax.rem(z + d, nz), y, core) for d in steps]

    barrier = pltpu.get_barrier_semaphore()
    for other in line + [across, sibling]:
        pl.semaphore_signal(barrier, inc=1, device_id={"row": other}, device_id_type=MESH)

    pair_copy = pltpu.make_async_copy(pair_hbm, pair_ref, pair_sem)
    final_copy = pltpu.make_async_copy(final_hbm, final_ref, final_sem)
    final_copy.start()
    pair_copy.start()

    x = x_ref[...].astype(jnp.float32).reshape(depth * res, channels)
    mean = jnp.mean(x, axis=-1, keepdims=True)
    centred = x - mean
    var = jnp.mean(centred * centred, axis=-1, keepdims=True)
    normed = centred * lax.rsqrt(var + 1e-05) * scale_ref[...][None, :] + shift_ref[...][None, :]
    for half in range(channels // LANES):
        normed_ref[half] = normed[:, half * LANES : (half + 1) * LANES]

    normed = jnp.concatenate(
        [
            jnp.concatenate(
                [normed_ref[half, pl.ds(j, depth, stride=res), :] for j in range(res)], axis=0
            )
            for half in range(channels // LANES)
        ],
        axis=1,
    ).astype(jnp.bfloat16)

    right = lax.dot_general(
        right_w_ref[...],
        normed,
        (((0,), (1,)), ((), ())),
        preferred_element_type=jnp.float32,
    )
    right = right + right_b_ref[...][:, None]
    right = right.astype(jnp.bfloat16).astype(jnp.float32)
    for block in range(res // pack):
        turned_ref[block] = right[:, block * LANES : (block + 1) * LANES]
    lane_block = lax.broadcasted_iota(jnp.int32, (high, LANES), 1) // depth
    for block in range(res // pack):
        parts = [turned_ref[block, pl.ds(low, high, stride=pack), :] for low in range(pack)]
        for j_low in range(pack):
            value = None
            for low in range(pack):
                moved = parts[low]
                if low != j_low:
                    moved = pltpu.roll(moved, ((low - j_low) % pack) * depth, 1)
                value = moved if value is None else jnp.where(lane_block == low, moved, value)
            j = block * pack + j_low
            rows_ref[pl.ds(j * high, high), :] = value
    cols_ref[me] = jnp.concatenate(
        [rows_ref[pl.ds(h, res, stride=high), :] for h in range(high)], axis=1
    ).astype(jnp.bfloat16)

    pl.semaphore_wait(barrier, nz + 1)
    sends = []

    def send(slot, target):
        copy = pltpu.make_async_remote_copy(
            src_ref=cols_ref.at[slot],
            dst_ref=cols_ref.at[slot],
            send_sem=send_sem.at[len(sends)],
            recv_sem=recv_sem.at[slot],
            device_id={"row": target},
            device_id_type=MESH,
        )
        copy.start()
        sends.append(copy)

    def arrived(slot):
        pltpu.make_async_remote_copy(
            src_ref=cols_ref.at[slot],
            dst_ref=cols_ref.at[slot],
            send_sem=send_sem.at[0],
            recv_sem=recv_sem.at[slot],
            device_id={"row": sibling},
            device_id_type=MESH,
        ).wait_recv()

    for target in line:
        send(me, target)
    send(me, across)
    send(me, sibling)

    left = jnp.dot(normed, left_w_ref[...], preferred_element_type=jnp.float32)
    left = (left + left_b_ref[...][None, :]).astype(jnp.bfloat16)
    final_copy.wait()
    final32_ref[...] = final_ref[...].astype(jnp.float32)

    def fold(e):
        matrix = jnp.concatenate(
            [final32_ref[pl.ds(e + k, width, stride=width), :] for k in range(2)], axis=1
        ).astype(jnp.bfloat16)
        part = jnp.dot(left, matrix, preferred_element_type=jnp.float32) * (1.0 / depth)
        part = part.astype(jnp.bfloat16)
        for k in range(2):
            for i in range(res):
                folded_ref[(e + k) * depth : (e + k + 1) * depth, i * cz : (i + 1) * cz] = part[
                    i * depth : (i + 1) * depth, k * cz : (k + 1) * cz
                ]

    for e in range(0, width // 2, 2):
        fold(e)
    for d in steps:
        slot = place(lax.rem(z + nz - d, nz), y, core)
        arrived(slot)
        send(slot, across)
        send(slot, sibling)
    for e in range(width // 2, width, 2):
        fold(e)
    for d in [0] + steps:
        slot = place(lax.rem(z + nz - d, nz), 1 - y, core)
        arrived(slot)
        send(slot, sibling)
    for y_ in range(2):
        for d in [0] + steps:
            arrived(place(lax.rem(z + nz - d, nz), y_, 1 - core))

    pair_copy.wait()
    cols = cols_ref[...].reshape(n_row * res, width * depth)
    outs = []
    for i in range(0, res, 2):
        update = jnp.dot(
            cols, folded_ref[:, i * cz : (i + 2) * cz], preferred_element_type=jnp.float32
        )
        for k in range(2):
            part = update[:, k * cz : (k + 1) * cz] + final_b_ref[...][None, :]
            out_ref[i + k] = (pair_ref[i + k].astype(jnp.float32) + part).astype(jnp.bfloat16)
        copy = pltpu.make_async_copy(
            out_ref.at[pl.ds(i, 2)], out_hbm.at[pl.ds(i, 2)], out_sem.at[i // 2]
        )
        copy.start()
        outs.append(copy)
    for copy in sends:
        copy.wait_send()
    for copy in outs:
        copy.wait()


def local(n_row, x, scale, shift, left_w, left_b, right_w, right_b, final_w, final_b, pair):
    depth, res, channels = x.shape
    width = left_w.shape[1]
    cz = final_w.shape[1]
    vmem = pl.BlockSpec(memory_space=pltpu.VMEM)
    hbm = pl.BlockSpec(memory_space=pl.ANY)
    return pl.pallas_call(
        functools.partial(kernel, n_row),
        out_shape=jax.ShapeDtypeStruct(pair.shape, pair.dtype),
        in_specs=[vmem] * 7 + [hbm, vmem, hbm],
        out_specs=hbm,
        scratch_shapes=[
            pltpu.VMEM((channels // LANES, depth * res, LANES), jnp.float32),
            pltpu.VMEM(final_w.shape, jnp.bfloat16),
            pltpu.VMEM(final_w.shape, jnp.float32),
            pltpu.VMEM((width * depth, res * cz), jnp.bfloat16),
            pltpu.VMEM((res * depth // LANES, width, LANES), jnp.float32),
            pltpu.VMEM((res * width * depth // LANES, LANES), jnp.float32),
            pltpu.VMEM((n_row, res, width * depth), jnp.bfloat16),
            pltpu.VMEM(pair.shape, jnp.bfloat16),
            pltpu.VMEM(pair.shape, jnp.bfloat16),
            pltpu.SemaphoreType.DMA,
            pltpu.SemaphoreType.DMA,
            pltpu.SemaphoreType.DMA((res // 2,)),
            pltpu.SemaphoreType.DMA((n_row - 1,)),
            pltpu.SemaphoreType.DMA((n_row,)),
        ],
        compiler_params=pltpu.CompilerParams(
            collective_id=0, has_side_effects=True, vmem_limit_bytes=48 * 1024 * 1024
        ),
    )(x, scale, shift, left_w, left_b, right_w, right_b, final_w, final_b, pair)


def solution(mesh):
    placed = (
        P("groups", "row", None),
        P(),
        P(),
        P(),
        P(),
        P(),
        P(),
        P(),
        P(),
        P(("groups", "row"), None, None),
    )
    return jax.shard_map(
        functools.partial(local, mesh.shape["row"]),
        mesh=mesh,
        in_specs=placed,
        out_specs=P(("groups", "row"), None, None),
        check_vma=False,
    )
```

```python
import functools

import jax
import jax.numpy as jnp
from jax import lax
from jax.experimental import pallas as pl
from jax.experimental.pallas import tpu as pltpu
from jax.sharding import PartitionSpec as P

MESH = pl.DeviceIdType.MESH
LANES = 128


def kernel(
    n_row,
    x_hbm,
    scale_hbm,
    shift_hbm,
    left_w_hbm,
    left_b_hbm,
    right_w_hbm,
    right_b_hbm,
    final_hbm,
    final_b_hbm,
    pair_hbm,
    out_hbm,
    x_ref,
    scale_ref,
    shift_ref,
    left_w_ref,
    left_b_ref,
    right_w_ref,
    right_b_ref,
    final_ref,
    final_b_ref,
    pair_ref,
    normed_ref,
    final32_ref,
    folded_ref,
    turned_ref,
    rows_ref,
    cols_ref,
    out_ref,
    load_sem,
    out_sem,
    send_sem,
    recv_sem,
):
    depth, res, channels = x_ref.shape
    width = left_w_ref.shape[0]
    cz = final_b_ref.shape[0]
    pack = LANES // depth
    high = width // pack

    loads = [
        pltpu.make_async_copy(source, target, load_sem.at[index])
        for index, (source, target) in enumerate(
            (
                (x_hbm, x_ref),
                (scale_hbm, scale_ref),
                (shift_hbm, shift_ref),
                (right_w_hbm, right_w_ref),
                (right_b_hbm, right_b_ref),
                (left_w_hbm, left_w_ref),
                (left_b_hbm, left_b_ref),
                (final_hbm, final_ref),
                (final_b_hbm, final_b_ref),
                (pair_hbm, pair_ref),
            )
        )
    ]
    for copy in loads:
        copy.start()

    me = lax.axis_index("row")
    core = lax.rem(me, 2)
    y = lax.rem(me // 2, 2)
    z = me // 4
    nz = n_row // 4

    def place(z_, y_, core_):
        return z_ * 4 + y_ * 2 + core_

    if nz == 4:
        half = z // 2
        near = 1 - (z + half * (3 - 2 * z))
        others = [t + half * (3 - 2 * t) for t in (near, 2, 3)]
    else:
        steps = sorted(range(1, nz), key=lambda d: (min(d, nz - d), d))
        others = [lax.rem(z + d, nz) for d in steps]
    across = place(z, 1 - y, core)
    sibling = place(z, y, 1 - core)
    line = [place(t, y, core) for t in others]

    barrier = pltpu.get_barrier_semaphore()
    for other in line + [across, sibling]:
        pl.semaphore_signal(barrier, inc=1, device_id={"row": other}, device_id_type=MESH)

    for copy in loads[:3]:
        copy.wait()
    x = x_ref[...].astype(jnp.float32).reshape(depth * res, channels)
    mean = jnp.mean(x, axis=-1, keepdims=True)
    centred = x - mean
    var = jnp.mean(centred * centred, axis=-1, keepdims=True)
    normed = centred * lax.rsqrt(var + 1e-05) * scale_ref[...][None, :] + shift_ref[...][None, :]
    for half in range(channels // LANES):
        normed_ref[half] = normed[:, half * LANES : (half + 1) * LANES]

    normed = jnp.concatenate(
        [
            jnp.concatenate(
                [normed_ref[half, pl.ds(j, depth, stride=res), :] for j in range(res)], axis=0
            )
            for half in range(channels // LANES)
        ],
        axis=1,
    ).astype(jnp.bfloat16)

    for copy in loads[3:5]:
        copy.wait()
    right = lax.dot_general(
        right_w_ref[...],
        normed,
        (((1,), (1,)), ((), ())),
        preferred_element_type=jnp.float32,
    )
    right = right + right_b_ref[...][:, None]
    right = right.astype(jnp.bfloat16).astype(jnp.float32)
    for block in range(res // pack):
        turned_ref[block] = right[:, block * LANES : (block + 1) * LANES]
    lane_block = lax.broadcasted_iota(jnp.int32, (high, LANES), 1) // depth
    for block in range(res // pack):
        parts = [turned_ref[block, pl.ds(low, high, stride=pack), :] for low in range(pack)]
        for j_low in range(pack):
            value = None
            for low in range(pack):
                moved = parts[low]
                if low != j_low:
                    moved = pltpu.roll(moved, ((low - j_low) % pack) * depth, 1)
                value = moved if value is None else jnp.where(lane_block == low, moved, value)
            j = block * pack + j_low
            rows_ref[pl.ds(j * high, high), :] = value
    cols_ref[me] = jnp.concatenate(
        [rows_ref[pl.ds(h, res, stride=high), :] for h in range(high)], axis=1
    ).astype(jnp.bfloat16)

    pl.semaphore_wait(barrier, nz + 1)
    sends = []

    def send(slot, target):
        copy = pltpu.make_async_remote_copy(
            src_ref=cols_ref.at[slot],
            dst_ref=cols_ref.at[slot],
            send_sem=send_sem.at[len(sends)],
            recv_sem=recv_sem.at[slot],
            device_id={"row": target},
            device_id_type=MESH,
        )
        copy.start()
        sends.append(copy)

    def arrived(slot):
        pltpu.make_async_remote_copy(
            src_ref=cols_ref.at[slot],
            dst_ref=cols_ref.at[slot],
            send_sem=send_sem.at[0],
            recv_sem=recv_sem.at[slot],
            device_id={"row": sibling},
            device_id_type=MESH,
        ).wait_recv()

    for target in line:
        send(me, target)
    send(me, across)
    send(me, sibling)

    for copy in loads[5:8]:
        copy.wait()
    left = lax.dot_general(
        normed,
        left_w_ref[...],
        (((1,), (1,)), ((), ())),
        preferred_element_type=jnp.float32,
    )
    left = (left + left_b_ref[...][None, :]).astype(jnp.bfloat16)
    final32_ref[...] = final_ref[...].astype(jnp.float32)

    def fold(e):
        matrix = jnp.concatenate(
            [final32_ref[pl.ds(e + k, width, stride=width), :] for k in range(2)], axis=1
        ).astype(jnp.bfloat16)
        part = jnp.dot(left, matrix, preferred_element_type=jnp.float32) * (1.0 / depth)
        part = part.astype(jnp.bfloat16)
        for k in range(2):
            for i in range(res):
                folded_ref[(e + k) * depth : (e + k + 1) * depth, i * cz : (i + 1) * cz] = part[
                    i * depth : (i + 1) * depth, k * cz : (k + 1) * cz
                ]

    for e in range(0, width // 2, 2):
        fold(e)
    for t in others:
        slot = place(t, y, core)
        arrived(slot)
        send(slot, across)
        send(slot, sibling)
    for e in range(width // 2, width, 2):
        fold(e)
    for t in [z] + others:
        slot = place(t, 1 - y, core)
        arrived(slot)
        send(slot, sibling)
    for y_ in range(2):
        for t in [z] + others:
            arrived(place(t, y_, 1 - core))

    for copy in loads[8:]:
        copy.wait()
    cols = cols_ref[...].reshape(n_row * res, width * depth)
    outs = []
    for i in range(0, res, 2):
        update = jnp.dot(
            cols, folded_ref[:, i * cz : (i + 2) * cz], preferred_element_type=jnp.float32
        )
        for k in range(2):
            part = update[:, k * cz : (k + 1) * cz] + final_b_ref[...][None, :]
            out_ref[i + k] = (pair_ref[i + k].astype(jnp.float32) + part).astype(jnp.bfloat16)
        copy = pltpu.make_async_copy(
            out_ref.at[pl.ds(i, 2)], out_hbm.at[pl.ds(i, 2)], out_sem.at[i // 2]
        )
        copy.start()
        outs.append(copy)
    for copy in sends:
        copy.wait_send()
    for copy in outs:
        copy.wait()


def local(n_row, x, scale, shift, left_w, left_b, right_w, right_b, final_w, final_b, pair):
    depth, res, channels = x.shape
    width = left_w.shape[1]
    cz = final_w.shape[1]
    hbm = pl.BlockSpec(memory_space=pltpu.HBM)
    args = (x, scale, shift, left_w.T, left_b, right_w.T, right_b, final_w, final_b, pair)
    return pl.pallas_call(
        functools.partial(kernel, n_row),
        out_shape=jax.ShapeDtypeStruct(pair.shape, pair.dtype),
        in_specs=[hbm] * len(args),
        out_specs=hbm,
        scratch_shapes=[pltpu.VMEM(arg.shape, arg.dtype) for arg in args]
        + [
            pltpu.VMEM((channels // LANES, depth * res, LANES), jnp.float32),
            pltpu.VMEM(final_w.shape, jnp.float32),
            pltpu.VMEM((width * depth, res * cz), jnp.bfloat16),
            pltpu.VMEM((res * depth // LANES, width, LANES), jnp.float32),
            pltpu.VMEM((res * width * depth // LANES, LANES), jnp.float32),
            pltpu.VMEM((n_row, res, width * depth), jnp.bfloat16),
            pltpu.VMEM(pair.shape, jnp.bfloat16),
            pltpu.SemaphoreType.DMA((len(args),)),
            pltpu.SemaphoreType.DMA((res // 2,)),
            pltpu.SemaphoreType.DMA((n_row - 1,)),
            pltpu.SemaphoreType.DMA((n_row,)),
        ],
        compiler_params=pltpu.CompilerParams(
            collective_id=0, has_side_effects=True, vmem_limit_bytes=63 * 1024 * 1024
        ),
    )(*args)


def solution(mesh):
    placed = (
        P("groups", "row", None),
        P(),
        P(),
        P(),
        P(),
        P(),
        P(),
        P(),
        P(),
        P(("groups", "row"), None, None),
    )
    return jax.shard_map(
        functools.partial(local, mesh.shape["row"]),
        mesh=mesh,
        in_specs=placed,
        out_specs=P(("groups", "row"), None, None),
        check_vma=False,
    )
```

```python
import functools

import jax
import jax.numpy as jnp
from jax import lax
from jax.experimental import pallas as pl
from jax.experimental.pallas import tpu as pltpu
from jax.sharding import PartitionSpec as P

MESH = pl.DeviceIdType.MESH
LANES = 128


def kernel(
    n_row,
    x_hbm,
    scale_hbm,
    shift_hbm,
    left_w_hbm,
    left_b_hbm,
    right_w_hbm,
    right_b_hbm,
    final_hbm,
    final_b_hbm,
    pair_hbm,
    out_ref,
    x_ref,
    scale_ref,
    shift_ref,
    left_w_ref,
    left_b_ref,
    right_w_ref,
    right_b_ref,
    final_ref,
    final_b_ref,
    pair_ref,
    normed_ref,
    final32_ref,
    folded_ref,
    turned_ref,
    rows_ref,
    cols_ref,
    load_sem,
    send_sem,
    recv_sem,
):
    depth, res, channels = x_ref.shape
    width = left_w_ref.shape[0]
    cz = final_b_ref.shape[0]
    pack = LANES // depth
    high = width // pack

    loads = [
        pltpu.make_async_copy(source, target, load_sem.at[index])
        for index, (source, target) in enumerate(
            (
                (x_hbm, x_ref),
                (scale_hbm, scale_ref),
                (shift_hbm, shift_ref),
                (right_w_hbm, right_w_ref),
                (right_b_hbm, right_b_ref),
                (left_w_hbm, left_w_ref),
                (left_b_hbm, left_b_ref),
                (final_hbm, final_ref),
                (final_b_hbm, final_b_ref),
                (pair_hbm, pair_ref),
            )
        )
    ]
    for copy in loads[:5]:
        copy.start()

    me = lax.axis_index("row")
    core = lax.rem(me, 2)
    y = lax.rem(me // 2, 2)
    z = me // 4
    nz = n_row // 4

    def place(z_, y_, core_):
        return z_ * 4 + y_ * 2 + core_

    if nz == 4:
        half = z // 2
        near = 1 - (z + half * (3 - 2 * z))
        others = [t + half * (3 - 2 * t) for t in (near, 2, 3)]
    else:
        steps = sorted(range(1, nz), key=lambda d: (min(d, nz - d), d))
        others = [lax.rem(z + d, nz) for d in steps]
    across = place(z, 1 - y, core)
    sibling = place(z, y, 1 - core)
    line = [place(t, y, core) for t in others]

    barrier = pltpu.get_barrier_semaphore()
    for other in line + [across, sibling]:
        pl.semaphore_signal(barrier, inc=1, device_id={"row": other}, device_id_type=MESH)

    for copy in loads[:3]:
        copy.wait()
    x = x_ref[...].astype(jnp.float32).reshape(depth * res, channels)
    mean = jnp.mean(x, axis=-1, keepdims=True)
    centred = x - mean
    var = jnp.mean(centred * centred, axis=-1, keepdims=True)
    normed = centred * lax.rsqrt(var + 1e-05) * scale_ref[...][None, :] + shift_ref[...][None, :]
    for half in range(channels // LANES):
        normed_ref[half] = normed[:, half * LANES : (half + 1) * LANES]

    normed = jnp.concatenate(
        [
            jnp.concatenate(
                [normed_ref[half, pl.ds(j, depth, stride=res), :] for j in range(res)], axis=0
            )
            for half in range(channels // LANES)
        ],
        axis=1,
    ).astype(jnp.bfloat16)

    for copy in loads[3:5]:
        copy.wait()
    right = lax.dot_general(
        right_w_ref[...],
        normed,
        (((1,), (1,)), ((), ())),
        preferred_element_type=jnp.float32,
    )
    right = right + right_b_ref[...][:, None]
    right = right.astype(jnp.bfloat16).astype(jnp.float32)
    for block in range(res // pack):
        turned_ref[block] = right[:, block * LANES : (block + 1) * LANES]
    lane_block = lax.broadcasted_iota(jnp.int32, (high, LANES), 1) // depth
    for block in range(res // pack):
        parts = [turned_ref[block, pl.ds(low, high, stride=pack), :] for low in range(pack)]
        for j_low in range(pack):
            value = None
            for low in range(pack):
                moved = parts[low]
                if low != j_low:
                    moved = pltpu.roll(moved, ((low - j_low) % pack) * depth, 1)
                value = moved if value is None else jnp.where(lane_block == low, moved, value)
            j = block * pack + j_low
            rows_ref[pl.ds(j * high, high), :] = value
    cols_ref[me] = jnp.concatenate(
        [rows_ref[pl.ds(h, res, stride=high), :] for h in range(high)], axis=1
    ).astype(jnp.bfloat16)

    for copy in loads[5:]:
        copy.start()
    pl.semaphore_wait(barrier, nz + 1)
    sends = []

    def send(slot, target):
        copy = pltpu.make_async_remote_copy(
            src_ref=cols_ref.at[slot],
            dst_ref=cols_ref.at[slot],
            send_sem=send_sem.at[len(sends)],
            recv_sem=recv_sem.at[slot],
            device_id={"row": target},
            device_id_type=MESH,
        )
        copy.start()
        sends.append(copy)

    def arrived(slot):
        pltpu.make_async_remote_copy(
            src_ref=cols_ref.at[slot],
            dst_ref=cols_ref.at[slot],
            send_sem=send_sem.at[0],
            recv_sem=recv_sem.at[slot],
            device_id={"row": sibling},
            device_id_type=MESH,
        ).wait_recv()

    for target in line:
        send(me, target)
    send(me, across)
    send(me, sibling)

    for copy in loads[5:8]:
        copy.wait()
    left = lax.dot_general(
        normed,
        left_w_ref[...],
        (((1,), (1,)), ((), ())),
        preferred_element_type=jnp.float32,
    )
    left = (left + left_b_ref[...][None, :]).astype(jnp.bfloat16)
    final32_ref[...] = final_ref[...].astype(jnp.float32)

    def fold(e):
        matrix = jnp.concatenate(
            [final32_ref[pl.ds(e + k, width, stride=width), :] for k in range(2)], axis=1
        ).astype(jnp.bfloat16)
        part = jnp.dot(left, matrix, preferred_element_type=jnp.float32) * (1.0 / depth)
        part = part.astype(jnp.bfloat16)
        for k in range(2):
            for i in range(res):
                folded_ref[(e + k) * depth : (e + k + 1) * depth, i * cz : (i + 1) * cz] = part[
                    i * depth : (i + 1) * depth, k * cz : (k + 1) * cz
                ]

    for e in range(0, width // 2, 2):
        fold(e)
    for t in others:
        slot = place(t, y, core)
        arrived(slot)
        send(slot, across)
        send(slot, sibling)
    for e in range(width // 2, width, 2):
        fold(e)
    for t in [z] + others:
        slot = place(t, 1 - y, core)
        arrived(slot)
        send(slot, sibling)
    for y_ in range(2):
        for t in [z] + others:
            arrived(place(t, y_, 1 - core))

    for copy in loads[8:]:
        copy.wait()
    cols = cols_ref[...].reshape(n_row * res, width * depth)
    for i in range(0, res, 2):
        update = jnp.dot(
            cols, folded_ref[:, i * cz : (i + 2) * cz], preferred_element_type=jnp.float32
        )
        for k in range(2):
            part = update[:, k * cz : (k + 1) * cz] + final_b_ref[...][None, :]
            out_ref[i + k] = (pair_ref[i + k].astype(jnp.float32) + part).astype(jnp.bfloat16)
    for copy in sends:
        copy.wait_send()


def local(n_row, x, scale, shift, left_w, left_b, right_w, right_b, final_w, final_b, pair):
    depth, res, channels = x.shape
    width = left_w.shape[1]
    cz = final_w.shape[1]
    vmem = pl.BlockSpec(memory_space=pltpu.VMEM)
    hbm = pl.BlockSpec(memory_space=pltpu.HBM)
    args = (x, scale, shift, left_w.T, left_b, right_w.T, right_b, final_w, final_b, pair)
    args = tuple(pltpu.with_memory_space_constraint(arg, pltpu.HBM) for arg in args)
    return pl.pallas_call(
        functools.partial(kernel, n_row),
        out_shape=jax.ShapeDtypeStruct(pair.shape, pair.dtype),
        in_specs=[hbm] * len(args),
        out_specs=vmem,
        scratch_shapes=[pltpu.VMEM(arg.shape, arg.dtype) for arg in args]
        + [
            pltpu.VMEM((channels // LANES, depth * res, LANES), jnp.float32),
            pltpu.VMEM(final_w.shape, jnp.float32),
            pltpu.VMEM((width * depth, res * cz), jnp.bfloat16),
            pltpu.VMEM((res * depth // LANES, width, LANES), jnp.float32),
            pltpu.VMEM((res * width * depth // LANES, LANES), jnp.float32),
            pltpu.VMEM((n_row, res, width * depth), jnp.bfloat16),
            pltpu.SemaphoreType.DMA((len(args),)),
            pltpu.SemaphoreType.DMA((n_row - 1,)),
            pltpu.SemaphoreType.DMA((n_row,)),
        ],
        compiler_params=pltpu.CompilerParams(
            collective_id=0, has_side_effects=True, vmem_limit_bytes=48 * 1024 * 1024
        ),
    )(*args)


def solution(mesh):
    placed = (
        P("groups", "row", None),
        P(),
        P(),
        P(),
        P(),
        P(),
        P(),
        P(),
        P(),
        P(("groups", "row"), None, None),
    )
    return jax.shard_map(
        functools.partial(local, mesh.shape["row"]),
        mesh=mesh,
        in_specs=placed,
        out_specs=P(("groups", "row"), None, None),
        check_vma=False,
    )
```

```python
import functools

import jax
import jax.numpy as jnp
from jax import lax
from jax.experimental import pallas as pl
from jax.experimental.pallas import tpu as pltpu
from jax.sharding import PartitionSpec as P

MESH = pl.DeviceIdType.MESH
LANES = 128


def kernel(
    n_row,
    x_hbm,
    scale_hbm,
    shift_hbm,
    left_w_hbm,
    left_b_hbm,
    right_w_hbm,
    right_b_hbm,
    final_hbm,
    final_b_hbm,
    pair_hbm,
    out_ref,
    x_ref,
    scale_ref,
    shift_ref,
    left_w_ref,
    left_b_ref,
    right_w_ref,
    right_b_ref,
    final_ref,
    final_b_ref,
    pair_ref,
    normed_ref,
    final32_ref,
    folded_ref,
    turned_ref,
    rows_ref,
    cols_ref,
    load_sem,
    send_sem,
    recv_sem,
):
    depth, res, channels = x_ref.shape
    width = left_w_ref.shape[0]
    cz = final_b_ref.shape[0]
    pack = LANES // depth
    high = width // pack

    loads = [
        pltpu.make_async_copy(source, target, load_sem.at[index])
        for index, (source, target) in enumerate(
            (
                (x_hbm, x_ref),
                (scale_hbm, scale_ref),
                (shift_hbm, shift_ref),
                (right_w_hbm, right_w_ref),
                (right_b_hbm, right_b_ref),
                (left_w_hbm, left_w_ref),
                (left_b_hbm, left_b_ref),
                (final_hbm, final_ref),
                (final_b_hbm, final_b_ref),
                (pair_hbm, pair_ref),
            )
        )
    ]
    for copy in loads[:5]:
        copy.start()

    me = lax.axis_index("row")
    core = lax.rem(me, 2)
    y = lax.rem(me // 2, 2)
    z = me // 4
    nz = n_row // 4

    def place(z_, y_, core_):
        return z_ * 4 + y_ * 2 + core_

    if nz == 4:
        half = z // 2
        near = 1 - (z + half * (3 - 2 * z))
        others = [t + half * (3 - 2 * t) for t in (near, 2, 3)]
    else:
        steps = sorted(range(1, nz), key=lambda d: (min(d, nz - d), d))
        others = [lax.rem(z + d, nz) for d in steps]
    across = place(z, 1 - y, core)
    sibling = place(z, y, 1 - core)
    corner = place(z, 1 - y, 1 - core)
    line = [place(t, y, core) for t in others]

    barrier = pltpu.get_barrier_semaphore()
    for other in line + [across, corner, sibling]:
        pl.semaphore_signal(barrier, inc=1, device_id={"row": other}, device_id_type=MESH)

    for copy in loads[:3]:
        copy.wait()
    x = x_ref[...].astype(jnp.float32).reshape(depth * res, channels)
    mean = jnp.mean(x, axis=-1, keepdims=True)
    centred = x - mean
    var = jnp.mean(centred * centred, axis=-1, keepdims=True)
    normed = centred * lax.rsqrt(var + 1e-05) * scale_ref[...][None, :] + shift_ref[...][None, :]
    for half in range(channels // LANES):
        normed_ref[half] = normed[:, half * LANES : (half + 1) * LANES]

    normed = jnp.concatenate(
        [
            jnp.concatenate(
                [normed_ref[half, pl.ds(j, depth, stride=res), :] for j in range(res)], axis=0
            )
            for half in range(channels // LANES)
        ],
        axis=1,
    ).astype(jnp.bfloat16)

    for copy in loads[3:5]:
        copy.wait()
    right = lax.dot_general(
        right_w_ref[...],
        normed,
        (((1,), (1,)), ((), ())),
        preferred_element_type=jnp.float32,
    )
    right = right + right_b_ref[...][:, None]
    right = right.astype(jnp.bfloat16).astype(jnp.float32)
    for block in range(res // pack):
        turned_ref[block] = right[:, block * LANES : (block + 1) * LANES]
    lane_block = lax.broadcasted_iota(jnp.int32, (high, LANES), 1) // depth
    for block in range(res // pack):
        parts = [turned_ref[block, pl.ds(low, high, stride=pack), :] for low in range(pack)]
        for j_low in range(pack):
            value = None
            for low in range(pack):
                moved = parts[low]
                if low != j_low:
                    moved = pltpu.roll(moved, ((low - j_low) % pack) * depth, 1)
                value = moved if value is None else jnp.where(lane_block == low, moved, value)
            j = block * pack + j_low
            rows_ref[pl.ds(j * high, high), :] = value
    cols_ref[me] = jnp.concatenate(
        [rows_ref[pl.ds(h, res, stride=high), :] for h in range(high)], axis=1
    ).astype(jnp.bfloat16)

    for copy in loads[5:]:
        copy.start()
    pl.semaphore_wait(barrier, nz + 2)
    sends = []

    def send(slot, target):
        copy = pltpu.make_async_remote_copy(
            src_ref=cols_ref.at[slot],
            dst_ref=cols_ref.at[slot],
            send_sem=send_sem.at[len(sends)],
            recv_sem=recv_sem.at[slot],
            device_id={"row": target},
            device_id_type=MESH,
        )
        copy.start()
        sends.append(copy)

    def arrived(slot):
        pltpu.make_async_remote_copy(
            src_ref=cols_ref.at[slot],
            dst_ref=cols_ref.at[slot],
            send_sem=send_sem.at[0],
            recv_sem=recv_sem.at[slot],
            device_id={"row": sibling},
            device_id_type=MESH,
        ).wait_recv()

    for target in line:
        send(me, target)
    for target in (across, corner, sibling):
        send(me, target)

    for copy in loads[5:8]:
        copy.wait()
    left = lax.dot_general(
        normed,
        left_w_ref[...],
        (((1,), (1,)), ((), ())),
        preferred_element_type=jnp.float32,
    )
    left = (left + left_b_ref[...][None, :]).astype(jnp.bfloat16)
    final32_ref[...] = final_ref[...].astype(jnp.float32)

    def fold(e):
        matrix = jnp.concatenate(
            [final32_ref[pl.ds(e + k, width, stride=width), :] for k in range(2)], axis=1
        ).astype(jnp.bfloat16)
        part = jnp.dot(left, matrix, preferred_element_type=jnp.float32) * (1.0 / depth)
        part = part.astype(jnp.bfloat16)
        for k in range(2):
            for i in range(res):
                folded_ref[(e + k) * depth : (e + k + 1) * depth, i * cz : (i + 1) * cz] = part[
                    i * depth : (i + 1) * depth, k * cz : (k + 1) * cz
                ]

    for e in range(0, width // 2, 2):
        fold(e)
    for t in others:
        slot = place(t, y, core)
        arrived(slot)
        for target in (across, corner, sibling):
            send(slot, target)
    for e in range(width // 2, width, 2):
        fold(e)
    for y_, core_ in ((y, 1 - core), (1 - y, core), (1 - y, 1 - core)):
        for t in [z] + others:
            arrived(place(t, y_, core_))

    for copy in loads[8:]:
        copy.wait()
    cols = cols_ref[...].reshape(n_row * res, width * depth)
    for i in range(0, res, 2):
        update = jnp.dot(
            cols, folded_ref[:, i * cz : (i + 2) * cz], preferred_element_type=jnp.float32
        )
        for k in range(2):
            part = update[:, k * cz : (k + 1) * cz] + final_b_ref[...][None, :]
            out_ref[i + k] = (pair_ref[i + k].astype(jnp.float32) + part).astype(jnp.bfloat16)
    for copy in sends:
        copy.wait_send()


def local(n_row, x, scale, shift, left_w, left_b, right_w, right_b, final_w, final_b, pair):
    depth, res, channels = x.shape
    width = left_w.shape[1]
    cz = final_w.shape[1]
    vmem = pl.BlockSpec(memory_space=pltpu.VMEM)
    hbm = pl.BlockSpec(memory_space=pltpu.HBM)
    args = (x, scale, shift, left_w.T, left_b, right_w.T, right_b, final_w, final_b, pair)
    args = tuple(pltpu.with_memory_space_constraint(arg, pltpu.HBM) for arg in args)
    return pl.pallas_call(
        functools.partial(kernel, n_row),
        out_shape=jax.ShapeDtypeStruct(pair.shape, pair.dtype),
        in_specs=[hbm] * len(args),
        out_specs=vmem,
        scratch_shapes=[pltpu.VMEM(arg.shape, arg.dtype) for arg in args]
        + [
            pltpu.VMEM((channels // LANES, depth * res, LANES), jnp.float32),
            pltpu.VMEM(final_w.shape, jnp.float32),
            pltpu.VMEM((width * depth, res * cz), jnp.bfloat16),
            pltpu.VMEM((res * depth // LANES, width, LANES), jnp.float32),
            pltpu.VMEM((res * width * depth // LANES, LANES), jnp.float32),
            pltpu.VMEM((n_row, res, width * depth), jnp.bfloat16),
            pltpu.SemaphoreType.DMA((len(args),)),
            pltpu.SemaphoreType.DMA((n_row - 1,)),
            pltpu.SemaphoreType.DMA((n_row,)),
        ],
        compiler_params=pltpu.CompilerParams(
            collective_id=0, has_side_effects=True, vmem_limit_bytes=48 * 1024 * 1024
        ),
    )(*args)


def solution(mesh):
    placed = (
        P("groups", "row", None),
        P(),
        P(),
        P(),
        P(),
        P(),
        P(),
        P(),
        P(),
        P(("groups", "row"), None, None),
    )
    return jax.shard_map(
        functools.partial(local, mesh.shape["row"]),
        mesh=mesh,
        in_specs=placed,
        out_specs=P(("groups", "row"), None, None),
        check_vma=False,
    )
```

```python
import functools

import jax
import jax.numpy as jnp
from jax import lax
from jax.experimental import pallas as pl
from jax.experimental.pallas import tpu as pltpu
from jax.sharding import PartitionSpec as P

MESH = pl.DeviceIdType.MESH
LANES = 128


def kernel(
    n_row,
    x_hbm,
    scale_hbm,
    shift_hbm,
    left_w_hbm,
    left_b_hbm,
    right_w_hbm,
    right_b_hbm,
    final_hbm,
    final_b_hbm,
    pair_hbm,
    out_ref,
    x_ref,
    scale_ref,
    shift_ref,
    left_w_ref,
    left_b_ref,
    right_w_ref,
    right_b_ref,
    final_ref,
    final_b_ref,
    pair_ref,
    normed_ref,
    final32_ref,
    folded_ref,
    turned_ref,
    rows_ref,
    cols_ref,
    load_sem,
    send_sem,
    recv_sem,
):
    depth, res, channels = x_ref.shape
    width = left_w_ref.shape[0]
    cz = final_b_ref.shape[0]
    pack = LANES // depth
    high = width // pack

    loads = [
        pltpu.make_async_copy(source, target, load_sem.at[index])
        for index, (source, target) in enumerate(
            (
                (x_hbm, x_ref),
                (scale_hbm, scale_ref),
                (shift_hbm, shift_ref),
                (right_w_hbm, right_w_ref),
                (right_b_hbm, right_b_ref),
                (left_w_hbm, left_w_ref),
                (left_b_hbm, left_b_ref),
                (final_hbm, final_ref),
                (final_b_hbm, final_b_ref),
                (pair_hbm, pair_ref),
            )
        )
    ]
    for copy in loads[:5]:
        copy.start()

    me = lax.axis_index("row")
    core = lax.rem(me, 2)
    y = lax.rem(me // 2, 2)
    z = me // 4
    nz = n_row // 4

    def place(z_, y_, core_):
        return z_ * 4 + y_ * 2 + core_

    if nz == 4:
        half = z // 2
        near = 1 - (z + half * (3 - 2 * z))
        others = [t + half * (3 - 2 * t) for t in (near, 2, 3)]
    else:
        steps = sorted(range(1, nz), key=lambda d: (min(d, nz - d), d))
        others = [lax.rem(z + d, nz) for d in steps]
    across = place(z, 1 - y, core)
    sibling = place(z, y, 1 - core)
    corner = place(z, 1 - y, 1 - core)
    line = [place(t, y, core) for t in others]

    barrier = pltpu.get_barrier_semaphore()
    for other in line + [across, corner, sibling]:
        pl.semaphore_signal(barrier, inc=1, device_id={"row": other}, device_id_type=MESH)

    for copy in loads[:3]:
        copy.wait()
    x = x_ref[...].astype(jnp.float32).reshape(depth * res, channels)
    mean = jnp.mean(x, axis=-1, keepdims=True)
    centred = x - mean
    var = jnp.mean(centred * centred, axis=-1, keepdims=True)
    normed = centred * lax.rsqrt(var + 1e-05) * scale_ref[...][None, :] + shift_ref[...][None, :]
    for half in range(channels // LANES):
        normed_ref[half] = normed[:, half * LANES : (half + 1) * LANES]

    normed = jnp.concatenate(
        [
            jnp.concatenate(
                [normed_ref[half, pl.ds(j, depth, stride=res), :] for j in range(res)], axis=0
            )
            for half in range(channels // LANES)
        ],
        axis=1,
    ).astype(jnp.bfloat16)

    for copy in loads[3:5]:
        copy.wait()
    right = lax.dot_general(
        right_w_ref[...],
        normed,
        (((1,), (1,)), ((), ())),
        preferred_element_type=jnp.float32,
    )
    right = right + right_b_ref[...][:, None]
    right = right.astype(jnp.bfloat16).astype(jnp.float32)
    for block in range(res // pack):
        turned_ref[block] = right[:, block * LANES : (block + 1) * LANES]
    lane_block = lax.broadcasted_iota(jnp.int32, (high, LANES), 1) // depth
    for block in range(res // pack):
        parts = [turned_ref[block, pl.ds(low, high, stride=pack), :] for low in range(pack)]
        for j_low in range(pack):
            value = None
            for low in range(pack):
                moved = parts[low]
                if low != j_low:
                    moved = pltpu.roll(moved, ((low - j_low) % pack) * depth, 1)
                value = moved if value is None else jnp.where(lane_block == low, moved, value)
            j = block * pack + j_low
            rows_ref[pl.ds(j * high, high), :] = value
    cols_ref[me] = jnp.concatenate(
        [rows_ref[pl.ds(h, res, stride=high), :] for h in range(high)], axis=1
    ).astype(jnp.bfloat16)

    for copy in loads[5:]:
        copy.start()
    pl.semaphore_wait(barrier, nz + 2)
    sends = []

    def send(slot, target):
        copy = pltpu.make_async_remote_copy(
            src_ref=cols_ref.at[slot],
            dst_ref=cols_ref.at[slot],
            send_sem=send_sem.at[len(sends)],
            recv_sem=recv_sem.at[slot],
            device_id={"row": target},
            device_id_type=MESH,
        )
        copy.start()
        sends.append(copy)

    def arrived(slot):
        pltpu.make_async_remote_copy(
            src_ref=cols_ref.at[slot],
            dst_ref=cols_ref.at[slot],
            send_sem=send_sem.at[0],
            recv_sem=recv_sem.at[slot],
            device_id={"row": sibling},
            device_id_type=MESH,
        ).wait_recv()

    for target in line:
        send(me, target)
    for target in (across, corner, sibling):
        send(me, target)

    for copy in loads[5:8]:
        copy.wait()
    left = lax.dot_general(
        normed,
        left_w_ref[...],
        (((1,), (1,)), ((), ())),
        preferred_element_type=jnp.float32,
    )
    left = (left + left_b_ref[...][None, :]).astype(jnp.bfloat16)
    final32_ref[...] = final_ref[...].astype(jnp.float32)

    def fold(e):
        matrix = jnp.concatenate(
            [final32_ref[pl.ds(e + k, width, stride=width), :] for k in range(2)], axis=1
        ).astype(jnp.bfloat16)
        part = jnp.dot(left, matrix, preferred_element_type=jnp.float32) * (1.0 / depth)
        part = part.astype(jnp.bfloat16)
        for k in range(2):
            for i in range(res):
                folded_ref[(e + k) * depth : (e + k + 1) * depth, i * cz : (i + 1) * cz] = part[
                    i * depth : (i + 1) * depth, k * cz : (k + 1) * cz
                ]

    for t in others:
        slot = place(t, y, core)
        arrived(slot)
        for target in (across, corner, sibling):
            send(slot, target)
    for e in range(0, width, 2):
        fold(e)
    for y_, core_ in ((y, 1 - core), (1 - y, core), (1 - y, 1 - core)):
        for t in [z] + others:
            arrived(place(t, y_, core_))

    for copy in loads[8:]:
        copy.wait()
    cols = cols_ref[...].reshape(n_row * res, width * depth)
    for i in range(0, res, 2):
        update = jnp.dot(
            cols, folded_ref[:, i * cz : (i + 2) * cz], preferred_element_type=jnp.float32
        )
        for k in range(2):
            part = update[:, k * cz : (k + 1) * cz] + final_b_ref[...][None, :]
            out_ref[i + k] = (pair_ref[i + k].astype(jnp.float32) + part).astype(jnp.bfloat16)
    for copy in sends:
        copy.wait_send()


def local(n_row, x, scale, shift, left_w, left_b, right_w, right_b, final_w, final_b, pair):
    depth, res, channels = x.shape
    width = left_w.shape[1]
    cz = final_w.shape[1]
    vmem = pl.BlockSpec(memory_space=pltpu.VMEM)
    hbm = pl.BlockSpec(memory_space=pltpu.HBM)
    args = (x, scale, shift, left_w.T, left_b, right_w.T, right_b, final_w, final_b, pair)
    args = tuple(pltpu.with_memory_space_constraint(arg, pltpu.HBM) for arg in args)
    return pl.pallas_call(
        functools.partial(kernel, n_row),
        out_shape=jax.ShapeDtypeStruct(pair.shape, pair.dtype),
        in_specs=[hbm] * len(args),
        out_specs=vmem,
        scratch_shapes=[pltpu.VMEM(arg.shape, arg.dtype) for arg in args]
        + [
            pltpu.VMEM((channels // LANES, depth * res, LANES), jnp.float32),
            pltpu.VMEM(final_w.shape, jnp.float32),
            pltpu.VMEM((width * depth, res * cz), jnp.bfloat16),
            pltpu.VMEM((res * depth // LANES, width, LANES), jnp.float32),
            pltpu.VMEM((res * width * depth // LANES, LANES), jnp.float32),
            pltpu.VMEM((n_row, res, width * depth), jnp.bfloat16),
            pltpu.SemaphoreType.DMA((len(args),)),
            pltpu.SemaphoreType.DMA((n_row - 1,)),
            pltpu.SemaphoreType.DMA((n_row,)),
        ],
        compiler_params=pltpu.CompilerParams(
            collective_id=0, has_side_effects=True, vmem_limit_bytes=48 * 1024 * 1024
        ),
    )(*args)


def solution(mesh):
    placed = (
        P("groups", "row", None),
        P(),
        P(),
        P(),
        P(),
        P(),
        P(),
        P(),
        P(),
        P(("groups", "row"), None, None),
    )
    return jax.shard_map(
        functools.partial(local, mesh.shape["row"]),
        mesh=mesh,
        in_specs=placed,
        out_specs=P(("groups", "row"), None, None),
        check_vma=False,
    )
```
